128 devices in a mesh: dp: 64 (over y, x, z_lo, core), tensor: 2 (over z_hi).
Axes of the slice: x: 4, y: 4, z: 4 (z_hi: 2, z_lo: 2; z = z_hi * 2 + z_lo), core: 2. Of those that a mesh axis runs over, the one named last changes fastest.
Arguments:
- block_input: bfloat16 [32768, 1536], P(('dp', 'tensor')), may hold values from -24 to 24
- cotangent: bfloat16 [32768, 1536], P(('dp', 'tensor')), may hold values from -24 to 24
- seg_ids: int32 [32768], P('dp'), may hold values from 0 to 6, as said below
- norm_gain: bfloat16 [1536], P(('dp', 'tensor')), may hold values from 0.25 to 1.75
- w_z: bfloat16 [1536, 3072], P('dp', 'tensor'), may hold values from -0.15625 to 0.15625
- w_x: bfloat16 [1536, 3072], P('dp', 'tensor'), may hold values from -0.15625 to 0.15625
- w_bc: bfloat16 [1536, 256], P(('dp', 'tensor')), may hold values from -0.15625 to 0.15625
- w_dt: bfloat16 [1536, 48], P('dp', 'tensor'), may hold values from -0.15625 to 0.15625
- conv_x_w: bfloat16 [4, 3072], P(None, 'tensor'), may hold values from -3 to 3
- conv_x_b: bfloat16 [3072], P('tensor'), may hold values from -3 to 3
- conv_bc_w: bfloat16 [4, 256], P(None, ('dp', 'tensor')), may hold values from -3 to 3
- conv_bc_b: bfloat16 [256], P(('dp', 'tensor')), may hold values from -3 to 3
- dt_bias: bfloat16 [48], P('tensor'), may hold values from -7 to -3
- a_log: bfloat16 [48], P('tensor'), may hold values from -1 to 1.5
- d_skip: bfloat16 [48], P('tensor'), may hold values from 0.5 to 1.5
- gate_gain: bfloat16 [3072], P('tensor'), may hold values from 0.25 to 1.75
- w_out: bfloat16 [3072, 1536], P('tensor', 'dp'), may hold values from -0.109375 to 0.109375
Outputs:
- out: bfloat16 [32768, 1536], P(('dp', 'tensor'))
- d_x: float32 [32768, 1536], P(('dp', 'tensor'))
- d_norm_gain: float32 [1536], P(('dp', 'tensor'))
- d_w_z: float32 [1536, 3072], P('dp', 'tensor')
- d_w_x: float32 [1536, 3072], P('dp', 'tensor')
- d_w_bc: float32 [1536, 256], P(('dp', 'tensor'))
- d_w_dt: float32 [1536, 48], P('dp', 'tensor')
- d_conv_x_w: float32 [4, 3072], P(None, 'tensor')
- d_conv_x_b: float32 [3072], P('tensor')
- d_conv_bc_w: float32 [4, 256], P(None, ('dp', 'tensor'))
- d_conv_bc_b: float32 [256], P(('dp', 'tensor'))
- d_dt_bias: float32 [48], P('tensor')
- d_a_log: float32 [48], P('tensor')
- d_d_skip: float32 [48], P('tensor')
- d_gate_gain: float32 [3072], P('tensor')
- d_w_out: float32 [3072, 1536], P('tensor', 'dp')
The draws below stay inside these ranges and needn't reach their ends.
Inputs may be any that keep to these rules, and one draw needn't show every extreme that they name: `seg_ids`: ids never fall along each sequence of 512 tokens and begin at 0 in each; the tokens at positions 255 and 256 of every sequence share an id; a new document can begin only within the first 32 positions of each aligned run of 64 tokens; in one sequence a document begins in every such run but the one at 256.
All inputs are finite; a program needn't handle non-finite values.
Results may differ from the reference program's by a relative error of at most 0.0093.
Values may be sent and summed in bfloat16 or wider, within the bound.
A program may use at most 192 MiB of HBM per device.

```python
import math
import jax
import jax.numpy as jnp
from jax import lax

D = 1536
HEADS = 48
HEAD_DIM = 64
STATE = 128
CONV = 4
SCAN_BLOCK = 256
DOC_MIN = 64
SEQ = 512
TOKENS = 32768


def draw_seg_ids(key, part):
    key = jax.random.fold_in(key, 11)
    seq_total = TOKENS // SEQ
    block_total = SEQ // DOC_MIN
    first_key, second_key, third_key = jax.random.split(key, 3)
    starting = jax.random.randint(first_key, (seq_total, block_total), 0, 3) == 0
    offsets = jax.random.randint(second_key, (seq_total, block_total), 0, max(1, DOC_MIN // 2))
    chosen = jax.random.randint(third_key, (), 0, seq_total)
    places = jnp.arange(block_total)
    rows_all = jnp.arange(seq_total)
    starting = starting | (rows_all == chosen)[:, None]
    starting = starting & (places != block_total // 2)[None, :] | (places == 0)[None, :]
    offsets = jnp.where((places == 0)[None, :], 0, offsets)
    positions = places[None, :] * DOC_MIN + offsets
    rows_index = jnp.broadcast_to(rows_all[:, None], positions.shape)
    marks = jnp.zeros((seq_total, SEQ), jnp.int32).at[rows_index, positions].add(starting.astype(jnp.int32))
    return (jnp.cumsum(marks, axis=1) - 1).reshape(TOKENS).astype(jnp.int32)


def strengthened(values, rng, source, target, shards_of, factor):
    def block_of(dim):
        return (jnp.arange(values.shape[dim]) // (values.shape[dim] // shards_of)).reshape((-1,) + (1,) * (values.ndim - 1 - dim))

    one_side = jax.random.permutation(rng, shards_of)[block_of(target)]
    far = (block_of(target) + shards_of // 2) % shards_of
    return jnp.where((block_of(source) == one_side) | (block_of(source) == far), factor * values, values)


def levels(stream_key, dims, cuts, smallest, high):
    factor_of = 1.0
    for axis_at, parts in cuts:
        draws = jax.random.uniform(jax.random.fold_in(jax.random.fold_in(stream_key, 6), axis_at), (parts,), jnp.float32, smallest / len(cuts), high / len(cuts))
        factor_of = factor_of * jnp.repeat(jnp.exp(draws), dims[axis_at] // parts).reshape((-1,) + (1,) * (len(dims) - 1 - axis_at))
    return factor_of


def scatter_about(key, shape, scale, most, cuts=(), held_as=jnp.bfloat16):
    values = scale * jax.random.normal(key, shape, jnp.float32)
    if cuts:
        values = values * levels(key, shape, cuts, -0.22, 0.18)
    return jnp.clip(values, -most, most).astype(held_as)


def gaussian_with(own_key, extent, deviation, most, shards, heavy, kind=jnp.bfloat16):
    values = deviation * jax.random.normal(own_key, extent, jnp.float32)
    if shards:
        values = values * levels(own_key, extent, shards, -0.22, 0.18)
    return jnp.clip(strengthened(values, jax.random.fold_in(own_key, 3), *heavy), -most, most).astype(kind)


def setup_inputs(seed: int = 0) -> dict:
    keys = jax.random.split(jax.random.key(seed), 18)
    return {
        "block_input": gaussian_with(keys[0], (TOKENS, D), 1.0, 24.0, ((0, 128),), (0, 1, 128, 5.5)),
        "cotangent": gaussian_with(keys[1], (TOKENS, D), 1.0, 24.0, ((0, 128),), (0, 1, 128, 5.5)),
        "seg_ids": draw_seg_ids(jax.random.fold_in(keys[17], 71), 0),
        "norm_gain": jnp.clip(1.0 + 0.15 * jax.random.normal(keys[3], (D,), jnp.float32), 0.25, 1.75).astype(jnp.bfloat16),
        "w_z": scatter_about(keys[4], (D, HEADS * HEAD_DIM), D ** -0.5, 0.15625, ((0, 64), (1, 2))),
        "w_x": scatter_about(keys[5], (D, HEADS * HEAD_DIM), D ** -0.5, 0.15625, ((0, 64), (1, 2))),
        "w_bc": scatter_about(keys[6], (D, 2 * STATE), D ** -0.5, 0.15625, ((0, 128),)),
        "w_dt": scatter_about(keys[7], (D, HEADS), D ** -0.5, 0.15625, ((0, 64), (1, 2))),
        "conv_x_w": scatter_about(keys[8], (CONV, HEADS * HEAD_DIM), CONV ** -0.5, 3.0, ((1, 2),)),
        "conv_x_b": scatter_about(keys[9], (HEADS * HEAD_DIM,), 0.5, 3.0, ((0, 2),)),
        "conv_bc_w": scatter_about(keys[10], (CONV, 2 * STATE), CONV ** -0.5, 3.0, ((1, 128),)),
        "conv_bc_b": scatter_about(keys[11], (2 * STATE,), 0.5, 3.0, ((0, 128),)),
        "dt_bias": jnp.clip(-7.0 + 4.0 * jax.random.uniform(keys[12], (HEADS,), jnp.float32) ** levels(keys[12], (HEADS,), ((0, 2),), -0.2, 0.2), -7.0, -3.0).astype(jnp.bfloat16),
        "a_log": jnp.clip(-1.0 + 2.5 * jax.random.uniform(keys[13], (HEADS,), jnp.float32) ** levels(keys[13], (HEADS,), ((0, 2),), -0.2, 0.2), -1.0, 1.5).astype(jnp.bfloat16),
        "d_skip": jnp.clip(0.5 + 1.0 * jax.random.uniform(keys[14], (HEADS,), jnp.float32) ** levels(keys[14], (HEADS,), ((0, 2),), -0.2, 0.2), 0.5, 1.5).astype(jnp.bfloat16),
        "gate_gain": jnp.clip(1.0 + 0.15 * jax.random.normal(keys[15], (HEADS * HEAD_DIM,), jnp.float32), 0.25, 1.75).astype(jnp.bfloat16),
        "w_out": scatter_about(keys[16], (HEADS * HEAD_DIM, D), (HEADS * HEAD_DIM) ** -0.5, 0.109375, ((0, 2), (1, 64))),
    }


EPS = 1e-05

@jax.custom_vjp
def low(v):
    return lax.optimization_barrier(v.astype(jnp.bfloat16)).astype(jnp.float32)

@jax.custom_vjp
def low_back(v):
    return v

def low_keep(v):
    return (low(v), None)

def low_pass(kept, grad):
    return (grad,)

def back_keep(v):
    return (v, None)

def back_low(kept, grad):
    return (low(grad),)
low.defvjp(low_keep, low_pass)
low_back.defvjp(back_keep, back_low)

def causal_conv(values, kernel, offsets, segments):
    length = values.shape[0]
    taps_count = kernel.shape[0]
    summed = offsets[None, :] + kernel[taps_count - 1][None, :] * values
    for distance in range(1, taps_count):
        shifted = jnp.pad(values, ((distance, 0), (0, 0)))[:length]
        same_doc = jnp.pad(segments, (distance, 0), constant_values=-1)[:length] == segments
        summed = summed + kernel[taps_count - 1 - distance][None, :] * shifted * same_doc[:, None].astype(values.dtype)
    return summed

def state_space(inputs_x, bc_vals, dt_raw, dt_bias, a_log, d_skip, segments):
    length = inputs_x.shape[0]
    head_count = dt_bias.shape[0]
    head_dim = inputs_x.shape[1] // head_count
    state_size = bc_vals.shape[1] // 2
    block_count = length // SCAN_BLOCK
    highest = lax.Precision.HIGHEST
    step_size = jax.nn.softplus(dt_raw + dt_bias)
    log_decay = step_size * -jnp.exp(a_log)
    values = inputs_x.reshape(block_count, SCAN_BLOCK, head_count, head_dim)
    write_map = bc_vals[:, :state_size].reshape(block_count, SCAN_BLOCK, state_size)
    read_map = bc_vals[:, state_size:].reshape(block_count, SCAN_BLOCK, state_size)
    step_rows = step_size.reshape(block_count, SCAN_BLOCK, head_count).transpose(0, 2, 1)
    cumulative = jnp.cumsum(log_decay.reshape(block_count, SCAN_BLOCK, head_count), axis=1).transpose(0, 2, 1)
    blocks = segments.reshape(block_count, SCAN_BLOCK)
    places = jnp.arange(SCAN_BLOCK)
    same_doc = (blocks[:, :, None] == blocks[:, None, :]) & (places[:, None] >= places[None, :])
    masked = same_doc[:, None]
    gap_sizes = cumulative[:, :, :, None] - cumulative[:, :, None, :]
    decays = jnp.where(masked, jnp.exp(jnp.where(masked, gap_sizes, 0.0)), 0.0)
    affinity = jnp.einsum('cin,cjn->cij', read_map, write_map, precision=highest)
    mixing = decays * affinity[:, None] * step_rows[:, :, None, :]
    within = jnp.einsum('chij,cjhp->cihp', mixing, values, precision=highest)
    finals = blocks[:, -1]
    tail_weight = jnp.exp(cumulative[:, :, -1:] - cumulative) * (blocks == finals[:, None]).astype(values.dtype)[:, None, :] * step_rows
    local_states = jnp.einsum('chj,cjn,cjhp->chnp', tail_weight, write_map, values, precision=highest)
    earlier = jnp.concatenate([jnp.full((1,), -1, finals.dtype), finals[:-1]])
    carried = (finals == earlier).astype(values.dtype)
    through = jnp.exp(cumulative[:, :, -1]) * carried[:, None]

    def advance(entering, pieces):
        factor, fresh_state = pieces
        return (factor[:, None, None] * entering + fresh_state, entering)
    start_state = jnp.zeros(local_states.shape[1:], values.dtype)
    unused, entering = lax.scan(advance, start_state, (through, local_states))
    enters = (blocks == earlier[:, None]).astype(values.dtype)
    entry_decay = jnp.exp(cumulative).transpose(0, 2, 1) * enters[:, :, None]
    across = jnp.einsum('cin,chnp->cihp', read_map, entering, precision=highest) * entry_decay[:, :, :, None]
    mixed_out = (within + across).reshape(length, head_count * head_dim)
    return mixed_out + inputs_x * jnp.repeat(d_skip, head_dim)

def block_forward(inputs, segments, norm_gain, w_z, w_x, w_bc, w_dt, conv_x_w, conv_x_b, conv_bc_w, conv_bc_b, dt_bias, a_log, d_skip, gate_gain, w_out):
    highest = lax.Precision.HIGHEST
    seq_count, length, model_width = inputs.shape
    inner_width = w_z.shape[1]
    state_twice = w_bc.shape[1]
    inv_rms = lax.rsqrt(lax.optimization_barrier(jnp.mean(inputs * inputs, axis=-1, keepdims=True)) + EPS)
    normed = low(inputs * inv_rms * norm_gain)
    w_all = jnp.concatenate([w_z, w_x, w_bc, w_dt], axis=1)
    proj = low_back(jnp.dot(normed.reshape(-1, model_width), w_all, precision=highest)).reshape(seq_count, length, -1)
    z_part = proj[..., :inner_width]
    x_pre = proj[..., inner_width:2 * inner_width]
    bc_pre = proj[..., 2 * inner_width:2 * inner_width + state_twice]
    dt_raw = proj[..., 2 * inner_width + state_twice:]
    conv_many = jax.vmap(causal_conv, in_axes=(0, None, None, 0))
    x_conv = jax.nn.silu(conv_many(x_pre, conv_x_w, conv_x_b, segments))
    bc_conv = jax.nn.silu(conv_many(bc_pre, conv_bc_w, conv_bc_b, segments))

    def one_sequence(items):
        return state_space(items[0], items[1], items[2], dt_bias, a_log, d_skip, items[3])
    mixer = lax.map(jax.checkpoint(one_sequence), (x_conv, bc_conv, dt_raw, segments))
    gated = mixer * jax.nn.silu(z_part)
    inv_gate = lax.rsqrt(lax.optimization_barrier(jnp.mean(gated * gated, axis=-1, keepdims=True)) + EPS)
    mixed = low(gated * inv_gate * gate_gain)
    branch = jnp.dot(mixed.reshape(-1, inner_width), w_out, precision=highest).reshape(seq_count, length, model_width)
    return inputs + branch

def reference(block_input, cotangent, seg_ids, norm_gain, w_z, w_x, w_bc, w_dt, conv_x_w, conv_x_b, conv_bc_w, conv_bc_b, dt_bias, a_log, d_skip, gate_gain, w_out):
    params = tuple((item.astype(jnp.float32) for item in (norm_gain, w_z, w_x, w_bc, w_dt, conv_x_w, conv_x_b, conv_bc_w, conv_bc_b, dt_bias, a_log, d_skip, gate_gain, w_out)))
    seq_total = TOKENS // SEQ
    per_step = math.gcd(seq_total, max(1, 4096 // SEQ))
    step_count = seq_total // per_step
    inputs = block_input.astype(jnp.float32).reshape(step_count, per_step, SEQ, D)
    cot_all = cotangent.astype(jnp.float32).reshape(step_count, per_step, SEQ, D)
    seg_all = seg_ids.reshape(step_count, per_step, SEQ)

    def step_fn(totals, items):
        x_block, cot_block, seg_block = items

        def forward(inputs_block, *weights):
            return block_forward(inputs_block, seg_block, *weights)
        result, pullback = jax.vjp(forward, x_block, *params)
        grads = pullback(cot_block)
        totals = tuple((total + grad for total, grad in zip(totals, grads[1:])))
        return (totals, (result.astype(jnp.bfloat16), grads[0]))
    zeros_all = tuple((jnp.zeros_like(item) for item in params))
    totals, (results, input_grads) = lax.scan(step_fn, zeros_all, (inputs, cot_all, seg_all))
    return (results.reshape(TOKENS, D), input_grads.reshape(TOKENS, D)) + totals
```

```python
import functools
import jax
import jax.numpy as jnp
from jax import lax
from jax.experimental import pallas as pl
from jax.experimental.pallas import tpu as pltpu
from jax.sharding import PartitionSpec as P

CONV = 4
SCAN_BLOCK = 256
EPS = 1e-05
MESH = pl.DeviceIdType.MESH
BF = jnp.bfloat16
F32 = jnp.float32

D = 1536
SEQ = 512
HALF = 768
WIDTHS = (256, 768, 768, 768)
STARTS = (0, 128, 512, 896)
PACKED = 1280


class Place:
    def __init__(self):
        dp = lax.axis_index("dp")
        tz = lax.axis_index("tensor")
        self.dp, self.tz = dp, tz
        self.core = dp % 2
        self.zlo = (dp // 2) % 2
        self.x = (dp // 4) % 4
        self.y = dp // 16
        c = self.core
        self.f = self.x * (1 - c) + self.y * c
        self.s = self.y * (1 - c) + self.x * c
        self.quad = dp % 4
        self.partner = (dp - c + (1 - c), tz)
        self.zmate = (dp - 2 * self.zlo + 2 * (1 - self.zlo), tz)

    def at(self, y, x, zlo, core, tz):
        return (((y * 4 + x) * 2 + zlo) * 2 + core, tz)

    def xy(self, dy, dx):
        return self.at((self.y + dy + 4) % 4, (self.x + dx + 4) % 4, self.zlo, self.core, self.tz)

    def first(self, d):
        c = self.core
        return self.xy(d * c, d * (1 - c))

    def second(self, d):
        c = self.core
        return self.xy(d * (1 - c), d * c)

    def member(self, r):
        return (self.dp - self.quad + (self.quad + r) % 4, self.tz)

    def ring(self, d):
        z = (self.tz * 2 + self.zlo + d + 4) % 4
        return self.at(self.y, self.x, z % 2, self.core, z // 2)

    def ring_half(self, d):
        return ((self.tz * 2 + self.zlo + d + 4) % 4) // 2

    def block(self, f, s):
        c = self.core
        return s * (1 - c) + f * c, f * (1 - c) + s * c

    def greet(self, more=False):
        barrier = pltpu.get_barrier_semaphore()
        others = [self.member(1), self.member(2), self.member(3)]
        others += [self.xy(0, 1), self.xy(0, -1), self.xy(1, 0), self.xy(-1, 0)]
        others += [self.ring(1), self.ring(-1)]
        if more:
            others += [self.xy(0, 2), self.xy(2, 0)]
        others += [self.ring(2)]
        for other in others:
            pl.semaphore_signal(barrier, inc=1, device_id=other, device_id_type=MESH)
        pl.semaphore_wait(barrier, len(others))


def send(src, dst, ssem, rsem, device):
    copy = pltpu.make_async_remote_copy(
        src_ref=src, dst_ref=dst, send_sem=ssem, recv_sem=rsem, device_id=device, device_id_type=MESH
    )
    copy.start()
    return copy


def wait_bytes(ref, sem):
    pltpu.make_async_copy(ref, ref, sem).wait()


class Gather:
    COUNT = 15

    def __init__(self, place, shard, stage, full, ssem, rsem, index):
        self.p, self.shard, self.stage, self.full = place, shard, stage, full
        self.ss = lambda k: ssem.at[index, k]
        self.rs = lambda k: rsem.at[index, k]
        self.lo = STARTS[index]
        self.width = WIDTHS[index]
        self.half = self.width // 2
        self.sent = []

    def cols(self):
        return pl.ds(self.lo, self.half)

    def start(self):
        p = self.p
        for r in (1, 2, 3):
            other_core = (p.quad + r) % 2
            self.sent.append(
                send(
                    self.shard.at[other_core, :, self.cols()],
                    self.stage.at[p.quad, :, self.cols()],
                    self.ss(r - 1),
                    self.rs(r - 1),
                    p.member(r),
                )
            )

    def first(self):
        p = self.p
        for copy in self.sent[:3]:
            copy.wait_recv()
        own = self.shard[p.core, :, self.lo : self.lo + self.half]
        rows = []
        for j in range(4):
            piece = jnp.where(p.quad == j, own, self.stage[j, :, self.lo : self.lo + self.half])
            piece = piece.astype(F32)
            rows.append(jnp.concatenate([piece[:24], piece[24:]], axis=1))
        self.full[p.core, p.y, p.x] = jnp.concatenate(rows, axis=0).astype(BF)
        block = self.full.at[p.core, p.y, p.x]
        self.sent.append(send(block, block, self.ss(3), self.rs(3), p.first(1)))
        self.sent.append(send(block, block, self.ss(4), self.rs(4), p.first(-1)))

    def first_far(self):
        p = self.p
        a, b = self.sent[3:5]
        a.wait_recv()
        yy, xx = p.block((p.f + 3) % 4, p.s)
        part = self.full.at[p.core, yy, xx, pl.ds(0, 48)]
        self.sent.append(send(part, part, self.ss(5), self.rs(5), p.first(1)))
        b.wait_recv()
        yy, xx = p.block((p.f + 1) % 4, p.s)
        part = self.full.at[p.core, yy, xx, pl.ds(48, 48)]
        self.sent.append(send(part, part, self.ss(6), self.rs(6), p.first(-1)))

    def _blocks(self, s, ks, k_sem, device):
        p = self.p
        for k in ks:
            yy, xx = p.block(k, s)
            part = self.full.at[p.core, yy, xx]
            send(part, part, self.ss(k_sem), self.rs(k_sem), device)

    def second(self):
        p = self.p
        for copy in self.sent[5:7]:
            copy.wait_recv()
        self._blocks(p.s, range(4), 7, p.second(1))
        self._blocks(p.s, range(4), 8, p.second(-1))
        self._blocks(p.s, range(4), 11, p.partner)

    def second_far(self):
        p = self.p
        wait_bytes(self.full.at[0, 0], self.rs(7))
        self._blocks((p.s + 3) % 4, (0, 1), 9, p.second(1))
        wait_bytes(self.full.at[0, 0], self.rs(8))
        self._blocks((p.s + 1) % 4, (2, 3), 10, p.second(-1))
        self._blocks((p.s + 3) % 4, range(4), 12, p.partner)
        self._blocks((p.s + 1) % 4, range(4), 13, p.partner)

    def last(self):
        p = self.p
        wait_bytes(self.full.at[0, 0, pl.ds(0, 2)], self.rs(9))
        wait_bytes(self.full.at[0, 0, pl.ds(0, 2)], self.rs(10))
        self._blocks((p.s + 2) % 4, range(4), 14, p.partner)

    def ready(self):
        for k in (11, 12, 13, 14):
            wait_bytes(self.full.at[0, 0], self.rs(k))

    def finish(self):
        for copy in self.sent:
            copy.wait_send()
        for k in (7, 8, 11, 12, 13, 14):
            wait_bytes(self.full.at[0, 0], self.ss(k))
        for k in (9, 10):
            wait_bytes(self.full.at[0, 0, pl.ds(0, 2)], self.ss(k))


class Cross:
    def __init__(self, place, relay, ssem, rsem, index):
        self.p, self.relay = place, relay
        self.ss = lambda k: ssem.at[index, k]
        self.rs = lambda k: rsem.at[index, k]

    def start(self, up, down):
        send(up, self.relay.at[0], self.ss(0), self.rs(0), self.p.ring(1))
        send(down, self.relay.at[1], self.ss(1), self.rs(1), self.p.ring(-1))

    def forward(self, up, down):
        p = self.p
        wait_bytes(self.relay.at[0], self.rs(0))
        send(self.relay.at[0], up(p.ring_half(-1)), self.ss(2), self.rs(2), p.ring(1))
        wait_bytes(self.relay.at[1], self.rs(1))
        send(self.relay.at[1], down(p.ring_half(1)), self.ss(3), self.rs(3), p.ring(-1))

    def ready(self):
        wait_bytes(self.relay.at[0], self.rs(2))
        wait_bytes(self.relay.at[1], self.rs(3))

    def release(self):
        wait_bytes(self.relay.at[0], self.ss(0))
        wait_bytes(self.relay.at[1], self.ss(1))

    def finish(self):
        wait_bytes(self.relay.at[0], self.ss(2))
        wait_bytes(self.relay.at[1], self.ss(3))


CHUNK = 256
HEADS = 4
TILE = 64
LOG2E = 1.4426950408889634
HIGH = lax.Precision.HIGHEST
NEVER = -1e30


def split(v):
    hi = v.astype(BF)
    return hi, (v - hi.astype(F32)).astype(BF)


def dot(a, b):
    return jnp.dot(a, b, preferred_element_type=F32)


def dot_nt(a, b):
    return lax.dot_general(a, b, (((1,), (1,)), ((), ())), preferred_element_type=F32)


def dot_tn(a, b):
    return lax.dot_general(a, b, (((0,), (0,)), ((), ())), preferred_element_type=F32)


def sig(v):
    return 0.5 * jnp.tanh(0.5 * v) + 0.5


def side(*parts):
    return jnp.concatenate(parts, axis=1)


def below(*parts):
    return jnp.concatenate(parts, axis=0)


def fine(product, a, b):
    a_hi, a_lo = split(a)
    b_hi, b_lo = split(b)
    if product is dot:
        return dot(side(a_hi, a_hi, a_lo), below(b_hi, b_lo, b_hi))
    if product is dot_nt:
        return dot_nt(side(a_hi, a_hi, a_lo), side(b_hi, b_lo, b_hi))
    return product(a_hi, b_hi) + (product(a_hi, b_lo) + product(a_lo, b_hi))


def lanes_in(width, low, high):
    lane = lax.broadcasted_iota(jnp.int32, (1, width), 1)
    return ((lane >= low) & (lane < high)).astype(F32)


def head_columns(table, c):
    turned = pltpu.roll(table, (128 - HEADS * c) % 128, 1)
    return [jnp.broadcast_to(turned[:, k : k + 1], table.shape) for k in range(HEADS)]


def on_channels(columns):
    lane = lax.broadcasted_iota(jnp.int32, columns[0].shape, 1)
    return side(jnp.where(lane < 64, columns[0], columns[1]), jnp.where(lane < 64, columns[2], columns[3]))


def head_of_channel(c):
    lane = lax.broadcasted_iota(jnp.int32, (CHUNK, 128), 0)
    head = lax.broadcasted_iota(jnp.int32, (CHUNK, 128), 1)
    return head - (HEADS * c + lane // 64)


def conv_pre(values, taps, same):
    summed = taps[4:5, :] + taps[3:4, :] * values
    for d in (1, 2, 3):
        summed = summed + taps[3 - d : 4 - d, :] * (pltpu.roll(values, d, 0) * same[:, d : d + 1])
    return summed


def slope_of(values, sigma):
    return sigma * (1.0 + values * (1.0 - sigma))


def doc_bias(b, segc, segr, flip):
    rows = segc[256 * b : 256 * b + 256, 0:1]
    cols = segr[0:1, 256 * b : 256 * b + 256]
    i = lax.broadcasted_iota(jnp.int32, (256, 256), 0)
    j = lax.broadcasted_iota(jnp.int32, (256, 256), 1)
    order = (j >= i) if flip else (i >= j)
    return jnp.where(order & (rows == cols), 0.0, NEVER)


def twice(column, width):
    return column if width == 128 else side(column, column)


def apart(values):
    return [values * lanes_in(CHUNK, 64 * k, 64 * k + 64).astype(BF) for k in range(HEADS)]


def packed(values, k, swapped, first, second):
    tile = slice(128 * (k // 2), 128 * (k // 2) + 128)
    left = lanes_in(128, 0, 64).astype(BF)
    right = lanes_in(128, 64, 128).astype(BF)
    here, there = (values, swapped) if k % 2 == 0 else (swapped, values)
    low = here[first][:, tile] * left
    return low if second is None else low + there[second][:, tile] * right


def swap(values):
    return side(pltpu.roll(values[:, 0:128], 64, 1), pltpu.roll(values[:, 128:256], 64, 1))


def tile(full, h, lo, width):
    value = full[h, :, :, :, pl.ds(lo, width)]
    return value.reshape(D, width)


def columns_of(c):
    return pl.ds(pl.multiple_of(c * CHUNK, CHUNK), CHUNK)


def front_kernel(
    wx_in, wz_in, wo_in, tiny, segr, chan_in, xin, cin,
    o_normed_t, o_cot_t, o_pre, o_z, o_gm, o_small, o_aux, o_ws, o_wx, o_wz, o_wo,
    o_xcp, o_y_low, o_sums, o_bcc, o_bc, o_cum, o_cum_t, o_step, o_same, o_segc, o_taps, o_chans, o_heads, o_mixed, o_normed_far, o_cot_far,
    shard, tiny_got, stage, w_s, w_x, w_z, w_o, x_all, c_all, relay_x, relay_c,
    normed, normed_t, cot_t, pre, zed, gm, small, aux,
    xcp, y, y_low, sums, bcc, bc, cum, cum_t, step, same, segc, taps, chans, heads,
    bias, affinity, b_t, sums_t, sums_got, pre_low, normed_far, cot_far,
    g_ssem, g_rsem, c_ssem, c_rsem, t_ssem, t_rsem, l_sem,
):
    p = Place()
    p.greet()
    gathers = [Gather(p, shard, stage, full, g_ssem, g_rsem, i) for i, full in enumerate((w_s, w_x, w_z, w_o))]
    gs, gx, gz, go = gathers
    cross_x = Cross(p, relay_x, c_ssem, c_rsem, 0)
    cross_c = Cross(p, relay_c, c_ssem, c_rsem, 1)
    local = []
    count = iter(range(32))

    def store(*pairs):
        for src, dst in pairs:
            copy = pltpu.make_async_copy(src, dst, l_sem.at[next(count)])
            copy.start()
            local.append(copy)

    def fold_in(value, lo):
        for h in range(2):
            left = value[:, HALF * h : HALF * h + 384]
            right = value[:, HALF * h + 384 : HALF * h + HALF]
            shard[h, :, lo : lo + 384] = jnp.concatenate([left, right], axis=0).astype(BF)

    tiny_copy = send(tiny.at[:, pl.ds(0, 384)], tiny_got, t_ssem.at[0], t_rsem.at[0], p.ring(2))
    fold_in(wx_in[...].astype(F32), STARTS[1])
    gx.start()
    cross_x.start(xin.at[pl.ds(0, 128)], xin.at[pl.ds(128, 128)])
    fold_in(wz_in[...].astype(F32), STARTS[2])
    gz.start()
    fold_in(wo_in[...].astype(F32), STARTS[3])
    go.start()
    tiny_copy.wait_recv()
    both = tiny[:, 0:384] + tiny_got[...]
    shard[0, :, 0:128] = jnp.concatenate([both[:, 0:128], tiny[:, 384:512]], axis=0).astype(BF)
    shard[1, :, 0:128] = jnp.concatenate([both[:, 128:256], both[:, 256:384]], axis=0).astype(BF)
    gs.start()
    cross_c.start(cin.at[pl.ds(0, 128)], cin.at[pl.ds(128, 128)])
    gx.first()
    gs.first()
    gx.first_far()
    gs.first_far()
    gx.second()
    gs.second()
    gz.first()
    go.first()
    x_all[p.tz] = xin[...]
    c_all[p.tz] = cin[...]

    ids = jnp.broadcast_to(segr[0:1, :], (128, SEQ)).T
    segc[...] = ids
    place = lax.broadcasted_iota(jnp.int32, (SEQ, 128), 0)
    lane = lax.broadcasted_iota(jnp.int32, (SEQ, 128), 1)
    table = jnp.where(lane == 4, (ids == ids[255:256]).astype(F32), jnp.where(lane == 0, 1.0, 0.0))
    for d in (1, 2, 3):
        close = (pltpu.roll(ids, d, 0) == ids) & (place >= d)
        table = jnp.where(lane == d, close.astype(F32), table)
    same[...] = table
    heads[...] = jnp.zeros_like(heads)
    heads[0:1, :] = chan_in[6:7, 0:128]
    heads[1:2, :] = jnp.where(lane[0:1] < 24, -jnp.exp(chan_in[6:7, 128:256]), 0.0)
    chans[...] = chan_in[...]
    skips = jnp.broadcast_to(chan_in[6:7, 256:384], (8, 128))
    for c in range(D // CHUNK):
        chans[6:7, CHUNK * c : CHUNK * c + CHUNK] = on_channels(head_columns(skips, c))[0:1]

    gs.second_far()
    gz.first_far()
    go.first_far()
    cross_x.forward(lambda t: x_all.at[t, pl.ds(0, 128)], lambda t: x_all.at[t, pl.ds(128, 128)])
    gs.last()
    gx.second_far()
    gz.second()
    gs.ready()
    column = w_s[1, :, :, :, 128:256].reshape(D, 128).astype(F32)
    aux[...] = column.T[:8]
    row = lax.broadcasted_iota(jnp.int32, (D, 256), 0)
    wide = lax.broadcasted_iota(jnp.int32, (D, 256), 1)
    pick = (row == 12 * (wide // 2) + wide % 2).astype(F32).astype(BF)
    found = dot(aux[...].astype(BF), pick)
    taps[...] = jnp.concatenate([found[1:6], jnp.zeros((3, 256), F32)], axis=0)
    cross_x.ready()
    gain = aux[0:1, :]

    @pl.loop(0, 32)
    def _(i):
        rows = x_all[i // 16, pl.ds(pl.multiple_of((i % 16) * 16, 16), 16), :].astype(F32)
        inv = lax.rsqrt(jnp.mean(rows * rows, axis=-1, keepdims=True) + EPS)
        normed[pl.ds(pl.multiple_of(i * 16, 16), 16), :] = (rows * inv * gain).astype(BF)

    gx.last()
    go.second()
    for h in range(2):
        small[:, 256 * h : 256 * h + 256] = dot(normed[...], tile(w_s, h, 0, 256))

    value = jnp.concatenate([small[:, 0:128], small[:, 256:384]], axis=1)
    value = conv_pre(value, taps, same)
    bcc[...] = value
    bc[...] = value * sig(value)
    raw = small[:, 128:256] + heads[0:1, :]
    soft = jnp.maximum(raw, 0.0) + jnp.log1p(jnp.exp(-jnp.abs(raw)))
    step[...] = soft
    decay = soft * heads[1:2, :]
    i = lax.broadcasted_iota(jnp.int32, (256, 256), 0)
    j = lax.broadcasted_iota(jnp.int32, (256, 256), 1)
    lower = (i >= j).astype(F32)
    for b in range(2):
        rows = slice(256 * b, 256 * b + 256)
        cum[rows, :] = LOG2E * jnp.dot(lower, decay[rows], precision=HIGH, preferred_element_type=F32)
        bias[b] = doc_bias(b, segc, segr, False)
        affinity[b] = fine(dot_nt, bc[rows, 128:256], bc[rows, 0:128])
    cum_turned = cum[...].T
    for h in range(24):
        cum_t[h] = cum_turned[h : h + 1]
    b_t[...] = bc[0:256, 0:128].T

    normed_t[...] = normed[...].astype(F32).T.astype(BF)
    store((normed_t, o_normed_t))
    give_normed = send(normed_t, normed_far, t_ssem.at[2], t_rsem.at[2], p.partner)
    gx.ready()

    def project(lhs, full, out):
        for h in range(2):
            @pl.loop(0, 3)
            def _(t):
                lo = pl.multiple_of(t * 256, 256)
                out[:, pl.ds(pl.multiple_of(h * HALF + t * 256, 256), 256)] = dot(lhs[...], tile(full, h, lo, 256))

    project(normed, w_x, pre)
    gz.second_far()
    cross_c.forward(lambda t: c_all.at[t, pl.ds(0, 128)], lambda t: c_all.at[t, pl.ds(128, 128)])
    store((w_s, o_ws), (w_x, o_wx), (small, o_small), (aux, o_aux), (bcc, o_bcc), (bc, o_bc), (cum, o_cum),
          (cum_t, o_cum_t), (step, o_step), (same, o_same), (segc, o_segc), (taps, o_taps), (chans, o_chans), (heads, o_heads))

    def scan_chunk(c):
        cols = columns_of(c)
        pre_low[:, cols] = pre[:, cols].astype(BF)
        value = conv_pre(pre[:, cols], chans[:, cols], same)
        xcp[:, cols] = value
        xc = value * sig(value)
        columns = head_columns(cum[...], c)
        cums = on_channels(columns)
        scaled = on_channels(head_columns(step[...], c)) * xc
        low, low_rest = split(scaled)
        x_hi, x_lo = apart(low), apart(low_rest)
        linked = same[:, 4:5]
        tail = jnp.exp2(cums[255:256] - cums[0:256]) * linked[0:256]
        state = fine(dot, b_t[...], tail * scaled[0:256])
        across = jnp.exp2(cums[256:512]) * linked[256:512] * fine(dot, bc[256:512, 128:256], state)
        for b in range(2):
            rows = slice(256 * b, 256 * b + 256)
            parts = []
            for k in range(HEADS):
                gap = twice(columns[k][rows], 256) - cum_t[HEADS * c + k, :, rows]
                parts.append(split(jnp.exp2(gap + bias[b]) * affinity[b]))
            m_hi = side(*[part[0] for part in parts])
            m_lo = side(*[part[1] for part in parts])
            both = dot(below(m_hi, m_lo), below(*[v[rows] for v in x_hi]))
            rest = both[256:512] + dot(m_hi, below(*[v[rows] for v in x_lo]))
            total = both[0:256]
            if b:
                total = total + across
            y_low[rows, cols] = total
            y[rows, cols] = total + rest

    pl.loop(0, 2)(scan_chunk)
    gz.last()
    go.second_far()
    pl.loop(2, 4)(scan_chunk)
    go.last()
    pl.loop(4, 6)(scan_chunk)
    store((xcp, o_xcp), (y_low, o_y_low), (pre_low, o_pre))
    pre_stored = local[-1]
    gz.ready()
    store((w_z, o_wz))
    project(normed, w_z, zed)
    store((zed, o_z))
    cross_c.ready()
    cot_t[...] = c_all[...].reshape(SEQ, D).astype(F32).T.astype(BF)
    store((cot_t, o_cot_t))
    give_cot = send(cot_t, cot_far, t_ssem.at[3], t_rsem.at[3], p.partner)
    go.ready()
    store((w_o, o_wo))
    project(c_all.reshape(SEQ, D), w_o, gm)
    store((gm, o_gm))

    @pl.loop(0, SEQ // 32)
    def _(i):
        rows = pl.ds(pl.multiple_of(i * 32, 32), 32)
        squares = jnp.zeros((32, CHUNK), F32)
        inner = jnp.zeros((32, CHUNK), F32)
        for c in range(D // CHUNK):
            cols = slice(CHUNK * c, CHUNK * c + CHUNK)
            value = xcp[rows, cols]
            gate = zed[rows, cols]
            total = y[rows, cols] + chans[6:7, cols] * (value * sig(value))
            gated = total * (gate * sig(gate))
            pre[rows, cols] = gated
            squares += gated * gated
            inner += gm[rows, cols] * chans[5:6, cols] * gated
        spot = lax.broadcasted_iota(jnp.int32, (32, 128), 1)
        first = jnp.sum(squares, axis=1, keepdims=True)
        second = jnp.sum(inner, axis=1, keepdims=True)
        sums[rows, :] = jnp.where(spot == 0, first, jnp.where(spot == 1, second, 0.0))

    give_normed.wait_recv()
    store((normed_far, o_normed_far))
    both_sums = sums[...]
    sums_t[...] = both_sums.T[:8]
    sums_copy = send(sums_t, sums_got, t_ssem.at[1], t_rsem.at[1], p.ring(2))
    for gather in gathers:
        gather.finish()
    for cross in (cross_x, cross_c):
        cross.release()
        cross.finish()
    sums_copy.wait_recv()
    total = jnp.concatenate([sums_t[...] + sums_got[...], jnp.zeros((120, SEQ), F32)], axis=0)
    sums[...] = total.T
    store((sums, o_sums))

    pre_stored.wait()
    local[:] = [copy for copy in local if copy is not pre_stored]

    @pl.loop(0, SEQ // 16)
    def _(i):
        rows = pl.ds(pl.multiple_of(i * 16, 16), 16)
        inv = lax.rsqrt(sums[rows, 0:1] * (1.0 / 3072) + EPS)
        pre_low[rows, :] = (pre[rows, :] * inv * chans[5:6, :]).astype(BF)

    store((pre_low, o_mixed))
    give_cot.wait_recv()
    store((cot_far, o_cot_far))
    give_normed.wait_send()
    give_cot.wait_send()
    tiny_copy.wait_send()
    sums_copy.wait_send()
    for copy in local:
        copy.wait()


def front(args):
    any_space = pl.BlockSpec(memory_space=pl.ANY)
    vmem = pl.BlockSpec(memory_space=pltpu.VMEM)
    wide = lambda w: ((2, 4, 4, 96, w), BF)
    full = ((SEQ, D), F32)
    rows = ((SEQ, 128), F32)
    turned = ((D, SEQ), BF)
    eight = ((8, D), F32)
    out_types = [
        turned, turned, ((SEQ, D), BF), full, full, ((SEQ, 512), F32), eight, wide(256), wide(HALF), wide(HALF), wide(HALF),
        full, full, rows, ((SEQ, 256), F32), ((SEQ, 256), F32), rows, ((24, 1, SEQ), F32), rows, rows, rows,
        ((8, 256), F32), eight, ((8, 128), F32), ((SEQ, D), BF), turned, turned,
    ]
    halves = ((2, 256, D), BF)
    relay = ((2, 128, D), BF)
    square = ((2, 256, 256), F32)
    scratch_types = [
        ((2, 48, PACKED), BF), ((24, 384), F32), ((4, 48, PACKED), BF), wide(256), wide(HALF), wide(HALF), wide(HALF),
        halves, halves, relay, relay,
        ((SEQ, D), BF), turned, turned, full, full, full, ((SEQ, 512), F32), eight,
        full, full, full, rows, ((SEQ, 256), F32), ((SEQ, 256), F32), rows, ((24, 1, SEQ), F32), rows, rows, rows,
        ((8, 256), F32), eight, ((8, 128), F32),
        square, square, ((128, 256), F32), ((8, SEQ), F32), ((8, SEQ), F32),
        ((SEQ, D), BF), turned, turned,
    ]
    sems = [(4, Gather.COUNT), (4, Gather.COUNT), (2, 4), (2, 4), (4,), (4,), (32,)]
    return pl.pallas_call(
        front_kernel,
        out_shape=[jax.ShapeDtypeStruct(*t) for t in out_types],
        in_specs=[vmem] * len(args),
        out_specs=[any_space] * len(out_types),
        scratch_shapes=[pltpu.VMEM(*t) for t in scratch_types] + [pltpu.SemaphoreType.DMA(s) for s in sems],
        compiler_params=pltpu.CompilerParams(
            collective_id=0, has_side_effects=True, vmem_limit_bytes=62 * 1024 * 1024
        ),
        cost_estimate=pl.CostEstimate(flops=2 * SEQ * D * 6000, bytes_accessed=60_000_000, transcendentals=8_000_000),
    )(*args)


class Scatter:
    COUNT = 11

    def __init__(self, place, lhs_t, lhs_far, rhs, rhs_far, width, own, bufs, result, ssem, rsem, index):
        self.p, self.lhs_t, self.lhs_far, self.rhs, self.rhs_far, self.width = place, lhs_t, lhs_far, rhs, rhs_far, width
        self.own, self.result = own, result
        self.rb1, self.rb2, self.ra1, self.ra2, self.zs, self.zr, self.keep, self.ds = bufs
        self.ss = lambda k: ssem.at[index, k]
        self.rs = lambda k: rsem.at[index, k]

    def give(self):
        p = self.p
        send(self.rhs(1 - p.core), self.rhs_far, self.ss(0), self.rs(0), p.partner)

    def own_half(self):
        p = self.p
        wait_bytes(self.rhs_far, self.rs(0))
        mine = self.rhs(p.core)

        @pl.loop(0, 2)
        def _(i):
            rows = pl.ds(pl.multiple_of(i * HALF, 128), HALF)
            both = side(self.lhs_t[rows, :], self.lhs_far[rows, :])
            places = pl.ds(2 * i, 2)
            for lo in range(0, self.width, 256):
                cols = slice(lo, lo + 256)
                value = dot(both, below(mine[:, cols], self.rhs_far[:, cols]))
                self.own[places, :, :, cols] = value.reshape(2, 4, 96, 256).astype(BF)

        far = (p.s + 2) % 4
        self._group(far, (0, 1), self.rb1.at[0], 1, p.second(1))
        self._group(far, (2, 3), self.rb1.at[1], 2, p.second(-1))

    def _group(self, s, ks, dst, k_sem, device):
        p = self.p
        for i, k in enumerate(ks):
            yy, xx = p.block(k, s)
            send(self.own.at[yy, xx], dst.at[i], self.ss(k_sem), self.rs(k_sem), device)

    def _add(self, f, s, terms):
        yy, xx = self.p.block(f, s)
        value = self.own[yy, xx].astype(F32)
        for term in terms:
            value = value + term.astype(F32)
        self.own[yy, xx] = value.astype(BF)

    def second(self):
        p = self.p
        wait_bytes(self.rb1.at[0], self.rs(1))
        for i, k in enumerate((0, 1)):
            self._add(k, (p.s + 1) % 4, [self.rb1[0, i]])
        self._group((p.s + 1) % 4, range(4), self.rb2.at[0], 3, p.second(1))
        wait_bytes(self.rb1.at[1], self.rs(2))
        for i, k in enumerate((2, 3)):
            self._add(k, (p.s + 3) % 4, [self.rb1[1, i]])
        self._group((p.s + 3) % 4, range(4), self.rb2.at[1], 4, p.second(-1))

    def first_far(self):
        p = self.p
        wait_bytes(self.rb2.at[0], self.rs(3))
        wait_bytes(self.rb2.at[1], self.rs(4))
        for k in range(4):
            self._add(k, p.s, [self.rb2[0, k], self.rb2[1, k]])
        yy, xx = p.block((p.f + 2) % 4, p.s)
        send(self.own.at[yy, xx, pl.ds(0, 48)], self.ra1.at[0], self.ss(5), self.rs(5), p.first(1))
        send(self.own.at[yy, xx, pl.ds(48, 48)], self.ra1.at[1], self.ss(6), self.rs(6), p.first(-1))

    def first(self):
        p = self.p
        wait_bytes(self.ra1.at[0], self.rs(5))
        yy, xx = p.block((p.f + 1) % 4, p.s)
        self.own[yy, xx, 0:48] = (self.own[yy, xx, 0:48].astype(F32) + self.ra1[0].astype(F32)).astype(BF)
        send(self.own.at[yy, xx], self.ra2.at[0], self.ss(7), self.rs(7), p.first(1))
        wait_bytes(self.ra1.at[1], self.rs(6))
        yy, xx = p.block((p.f + 3) % 4, p.s)
        self.own[yy, xx, 48:96] = (self.own[yy, xx, 48:96].astype(F32) + self.ra1[1].astype(F32)).astype(BF)
        send(self.own.at[yy, xx], self.ra2.at[1], self.ss(8), self.rs(8), p.first(-1))

    def beside(self):
        p = self.p
        wait_bytes(self.ra2.at[0], self.rs(7))
        wait_bytes(self.ra2.at[1], self.rs(8))
        yy, xx = p.block(p.f, p.s)
        value = self.own[yy, xx].astype(F32) + self.ra2[0].astype(F32) + self.ra2[1].astype(F32)
        self.zs[...] = jnp.where(p.zlo == 0, value[48:], value[:48]).astype(BF)
        self.keep[...] = jnp.where(p.zlo == 0, value[:48], value[48:])
        send(self.zs, self.zr, self.ss(9), self.rs(9), p.zmate)

    def home(self):
        p = self.p
        wait_bytes(self.zr, self.rs(9))
        value = self.keep[...] + self.zr[...].astype(F32)
        mine = pl.ds(pl.multiple_of(p.core * self.width, 128), self.width)
        self.result[:, mine] = jnp.where(p.core == 0, value[:24], value[24:])
        self.ds[...] = jnp.where(p.core == 0, value[24:], value[:24])
        send(self.ds, self.result.at[:, mine], self.ss(10), self.rs(10), p.partner)

    def finish(self):
        wait_bytes(self.ds, self.rs(10))
        wait_bytes(self.rhs_far, self.ss(0))
        for k in (5, 6):
            wait_bytes(self.ra1.at[0], self.ss(k))
        for k in (7, 8):
            wait_bytes(self.ra2.at[0], self.ss(k))
        wait_bytes(self.zs, self.ss(9))
        wait_bytes(self.ds, self.ss(10))
        for k in (1, 2):
            wait_bytes(self.rb1.at[0], self.ss(k))
        for k in (3, 4):
            wait_bytes(self.rb2.at[0], self.ss(k))


class Total:
    COUNT = 9

    def __init__(self, place, steps, slots, ssem, rsem, index, tensor):
        p = place
        self.steps, self.slots = steps, slots
        self.ss = lambda k: ssem.at[index, k]
        self.rs = lambda k: rsem.at[index, k]
        self.partners = [
            [p.partner], [p.zmate], [p.xy(0, 1), p.xy(0, 2), p.xy(0, 3)], [p.xy(1, 0), p.xy(2, 0), p.xy(3, 0)],
        ]
        if tensor:
            self.partners.append([p.ring(2)])
        self.sent = []
        self.at = 0

    def start(self):
        at = len(self.sent)
        for device in self.partners[self.at]:
            copy = send(self.steps.at[self.at], self.slots.at[at], self.ss(at), self.rs(at), device)
            self.sent.append(copy)
            at += 1
        self.at += 1

    def take(self):
        count = len(self.partners[self.at - 1])
        value = self.steps[self.at - 1]
        for i in range(len(self.sent) - count, len(self.sent)):
            self.sent[i].wait_recv()
            value = value + self.slots[i]
        self.steps[self.at] = value

    def step(self):
        self.take()
        self.start()

    def finish(self):
        for copy in self.sent:
            copy.wait_send()


def bufs(w):
    return [
        pltpu.VMEM((2, 2, 96, w), BF), pltpu.VMEM((2, 4, 96, w), BF),
        pltpu.VMEM((2, 48, w), BF), pltpu.VMEM((2, 96, w), BF), pltpu.VMEM((48, w), BF), pltpu.VMEM((48, w), BF),
        pltpu.VMEM((48, w), F32), pltpu.VMEM((24, w), F32),
    ]


def scan_backward_kernel(
    x_pre, z, gm, xcp, y_low, sums, small, same, segc, segr, chans, heads, bc, cum_in, cum_t, step_in,
    h_mixed, h_cot_t, h_cot_far, h_wo, h_xin,
    o_gz, o_gx, o_vec, o_gbc, o_gdt, o_heads, o_dwo, o_out,
    mixed, cot_t, cot_far, w_o, xin, far_o, own, bufs_o, result, peer_out, relay_out, got_out, own_out,
    s_ssem, s_rsem, c_ssem, c_rsem, l_sem,
    bias, affinity, b_t, c_t, d_aff, d_b, d_c, d_sums, d_last,
):
    c = pl.program_id(0)
    p = Place()
    columns_at = lambda h: mixed.at[:, pl.ds(pl.multiple_of(h * HALF, 128), HALF)]
    so = Scatter(p, cot_t, cot_far, columns_at, far_o, HALF, own, bufs_o, result, s_ssem, s_rsem, 0)
    cross_out = Cross(p, relay_out, c_ssem, c_rsem, 0)
    loads = [
        pltpu.make_async_copy(src, dst, l_sem.at[i])
        for i, (src, dst) in enumerate(((h_mixed, mixed), (h_cot_t, cot_t), (h_cot_far, cot_far), (h_wo, w_o), (h_xin, xin)))
    ]

    @pl.when(c == 0)
    def _():
        for load in loads:
            load.start()
        p.greet()
        loads[0].wait()
        so.give()

    @pl.when(c == 1)
    def _():
        loads[1].wait()
        loads[2].wait()
        so.own_half()

    @pl.when(c == 2)
    def _():
        so.second()
        loads[3].wait()

        @pl.loop(0, 4)
        def _(yy):
            value = dot_nt(mixed[:, 0:HALF], w_o[0, yy].reshape(384, HALF))
            value += dot_nt(mixed[:, HALF:D], w_o[1, yy].reshape(384, HALF))
            cols = pl.ds(pl.multiple_of(yy * 384, 128), 384)
            low, high = value[0:256], value[256:512]
            own_out[:, cols] = jnp.where(p.tz == 0, low, high)
            peer_out[:, cols] = jnp.where(p.tz == 0, high, low).astype(BF)

        cross_out.start(peer_out.at[pl.ds(0, 128)], peer_out.at[pl.ds(128, 128)])

    @pl.when(c == 3)
    def _():
        so.first_far()

    @pl.when(c == 4)
    def _():
        so.first()
        cross_out.forward(lambda t: got_out.at[pl.ds(0, 128)], lambda t: got_out.at[pl.ds(128, 128)])

    @pl.when(c == 5)
    def _():
        so.beside()

    @pl.when(c == 0)
    def _():
        for b in range(2):
            rows = slice(256 * b, 256 * b + 256)
            bias[b] = doc_bias(b, segc, segr, True)
            affinity[b] = fine(dot_nt, bc[rows, 0:128], bc[rows, 128:256])
        b_t[...] = bc[0:256, 0:128].T
        c_t[...] = bc[256:512, 128:256].T
        for ref in (d_aff, d_b, d_c, d_sums, d_last):
            ref[...] = jnp.zeros_like(ref)

    inv = lax.rsqrt(sums[:, 0:1] * (1.0 / 3072) + EPS)
    pull = inv * inv * inv * sums[:, 1:2] * (1.0 / 3072)
    gate = z[...]
    sigma = jax.nn.sigmoid(gate)
    act = gate * sigma
    pre = xcp[...]
    sigma_x = jax.nn.sigmoid(pre)
    xc = pre * sigma_x
    y = y_low[...] + chans[6:7, :] * xc
    gated = y * act
    unit = gated * inv
    gain = chans[5:6, :]
    grad_mixed = gm[...]
    o_vec[5:6, :] = jnp.sum(grad_mixed * unit, axis=0, keepdims=True)
    grad = inv * (grad_mixed * gain) - gated * pull
    gy = grad * act
    o_gz[...] = (grad * y * slope_of(gate, sigma)).astype(BF)
    o_vec[6:7, :] = jnp.sum(gy * xc, axis=0, keepdims=True)
    o_vec[7:8, :] = jnp.zeros((1, CHUNK), F32)
    columns = head_columns(cum_in[...], c)
    cum = on_channels(columns)
    step = on_channels(head_columns(step_in[...], c))
    scaled = step * xc
    x_parts, g_parts = split(scaled), split(gy)
    low, gy_low = x_parts[0], g_parts[0]
    x_swapped, g_swapped = split(swap(scaled)), split(swap(gy))
    alone = apart(gy_low)
    left = [side(packed(x_parts, k, x_swapped, 0, 1), packed(x_parts, k, x_swapped, 0, None)) for k in range(HEADS)]
    right = [side(packed(g_parts, k, g_swapped, 0, 0), packed(g_parts, k, g_swapped, 1, None)) for k in range(HEADS)]
    pieces = []
    for b in range(2):
        base = 256 * b
        rows = slice(base, base + 256)
        parts = []
        spot = jnp.zeros((256, 256), F32)
        for k in range(HEADS):
            gap = cum_t[HEADS * c + k, :, rows] - twice(columns[k][rows], 256)
            decay = jnp.exp2(gap + bias[b])
            parts.append((decay * affinity[b]).astype(BF))
            spot += decay * dot_nt(left[k][rows], right[k][rows])
        d_aff[b] += spot
        pieces.append(dot(side(*parts), below(*[v[rows] for v in alone])))
    linked = same[:, 4:5]
    tail = jnp.exp2(cum[255:256] - cum[0:256]) * linked[0:256]
    sent = tail * scaled[0:256]
    state = fine(dot, b_t[...], sent)
    read = jnp.exp2(cum[256:512]) * linked[256:512] * gy[256:512]
    d_state = fine(dot, c_t[...], read)
    by_state = tail * dot(bc[0:256, 0:128].astype(BF), d_state.astype(BF))
    d_b[0:256, :] += fine(dot_nt, sent, d_state)
    d_c[256:512, :] += fine(dot_nt, read, state)
    low_f = low.astype(F32)
    place = head_of_channel(c)
    pick = (place == 0).astype(F32).astype(BF)
    pick_far = (place == 64).astype(F32).astype(BF)
    ends = jnp.broadcast_to(jnp.sum(low_f[0:256] * by_state, axis=0, keepdims=True), (8, CHUNK))
    d_last[...] += dot(side(*split(ends)), below(pick, pick))
    d_scaled = below(pieces[0], pieces[1]) + below(by_state, jnp.zeros((256, CHUNK), F32))
    moments = side(*split(gy_low.astype(F32) * y_low[...] - low_f * d_scaled), *split(xc * d_scaled))
    d_sums[...] += dot(moments, below(pick, pick, pick_far, pick_far))
    gp = (step * d_scaled + chans[6:7, :] * gy) * slope_of(pre, sigma_x)
    values = x_pre[...].astype(F32)
    summed = chans[3:4, :] * gp
    o_vec[3:4, :] = jnp.sum(gp * values, axis=0, keepdims=True)
    o_vec[4:5, :] = jnp.sum(gp, axis=0, keepdims=True)
    for d in (1, 2, 3):
        moved = pltpu.roll(gp * same[:, d : d + 1], SEQ - d, 0)
        summed = summed + chans[3 - d : 4 - d, :] * moved
        o_vec[3 - d : 4 - d, :] = jnp.sum(moved * values, axis=0, keepdims=True)
    o_gx[...] = summed.astype(BF)

    @pl.when(c == pl.num_programs(0) - 1)
    def _():
        i = lax.broadcasted_iota(jnp.int32, (256, 256), 0)
        j = lax.broadcasted_iota(jnp.int32, (256, 256), 1)
        upper = (j >= i).astype(F32)
        lane = lax.broadcasted_iota(jnp.int32, (256, 128), 1)
        d_sums[255:256, :] += d_last[0:1, :]
        d_step = pltpu.roll(d_sums[...], 64, 1)
        rate = heads[1:2, :]
        raw = small[...] + heads[0:1, :]
        slope = jax.nn.sigmoid(raw)
        bias_sum = jnp.zeros((1, 128), F32)
        rate_sum = jnp.zeros((1, 128), F32)
        for b in range(2):
            rows = slice(256 * b, 256 * b + 256)
            o_gbc[rows, 0:128] = d_b[rows] + fine(dot, d_aff[b], bc[rows, 128:256])
            o_gbc[rows, 128:256] = d_c[rows] + fine(dot_tn, d_aff[b], bc[rows, 0:128])
            d_log = jnp.dot(upper, d_sums[rows], precision=HIGH, preferred_element_type=F32)
            grad_raw = (d_step[rows] + rate * d_log) * slope[rows]
            grad_raw = jnp.where(lane < 24, grad_raw, 0.0)
            o_gdt[rows] = grad_raw.astype(BF)
            bias_sum += jnp.sum(grad_raw, axis=0, keepdims=True)
            rate_sum += jnp.sum(d_log * step_in[rows] * rate, axis=0, keepdims=True)
        o_heads[...] = jnp.zeros_like(o_heads)
        o_heads[0:1, :] = bias_sum
        o_heads[1:2, :] = rate_sum
        so.home()
        cross_out.ready()
        cross_out.release()
        loads[4].wait()
        for i in range(8):
            part = slice(32 * i, 32 * i + 32)
            peer_out[part, :] = (xin[part, :].astype(F32) + own_out[part, :] + got_out[part, :].astype(F32)).astype(BF)
        so.finish()
        cross_out.finish()
        stores = [pltpu.make_async_copy(result, o_dwo, l_sem.at[5]), pltpu.make_async_copy(peer_out, o_out, l_sem.at[6])]
        for copy in stores:
            copy.start()
        for copy in stores:
            copy.wait()


def block_spec(shape):
    if len(shape) == 3:
        return pl.BlockSpec(shape, lambda c: (0, 0, 0))
    rows, width = shape
    if width == SEQ and rows == SEQ:
        return pl.BlockSpec((rows, 128), lambda c: (0, 1))
    if width == D:
        return pl.BlockSpec((rows, CHUNK), lambda c: (0, c))
    return pl.BlockSpec((rows, width), lambda c: (0, 0))


def scan_backward(args, far):
    sds = jax.ShapeDtypeStruct
    outs = [
        sds((SEQ, D), BF), sds((SEQ, D), BF), sds((8, D), F32), sds((SEQ, 256), F32), sds((SEQ, 128), BF), sds((8, 128), F32),
    ]
    far_outs = [sds((24, D), F32), sds((256, D), BF)]
    half = pltpu.VMEM((4, 4, 96, HALF), BF)
    wide = lambda n, t: pltpu.VMEM((n, D), t)
    square = pltpu.VMEM((2, 256, 256), F32)
    rows = pltpu.VMEM((SEQ, 128), F32)
    scratch = [
        wide(SEQ, BF), pltpu.VMEM((D, SEQ), BF), pltpu.VMEM((D, SEQ), BF), pltpu.VMEM((2, 4, 4, 96, HALF), BF), wide(256, BF),
        pltpu.VMEM((SEQ, HALF), BF), half, bufs(HALF),
        wide(24, F32), wide(256, BF), pltpu.VMEM((2, 128, D), BF), wide(256, BF), wide(256, F32),
        pltpu.SemaphoreType.DMA((1, Scatter.COUNT)), pltpu.SemaphoreType.DMA((1, Scatter.COUNT)),
        pltpu.SemaphoreType.DMA((1, 4)), pltpu.SemaphoreType.DMA((1, 4)), pltpu.SemaphoreType.DMA((7,)),
        square, square, pltpu.VMEM((128, 256), F32), pltpu.VMEM((128, 256), F32), square, rows, rows, rows,
        pltpu.VMEM((8, 128), F32),
    ]
    any_space = pl.BlockSpec(memory_space=pl.ANY)
    return pl.pallas_call(
        scan_backward_kernel,
        grid=(D // CHUNK,),
        out_shape=outs + far_outs,
        in_specs=[block_spec(a.shape) for a in args] + [any_space] * len(far),
        out_specs=[block_spec(o.shape) for o in outs] + [any_space] * len(far_outs),
        scratch_shapes=scratch,
        compiler_params=pltpu.CompilerParams(collective_id=2, has_side_effects=True, vmem_limit_bytes=62 * 1024 * 1024),
        cost_estimate=pl.CostEstimate(flops=8_000_000_000, bytes_accessed=30_000_000, transcendentals=5_000_000),
    )(*args, *far)


def back_kernel(
    h_normed_t, h_normed_far, h_gz, h_gx, h_gdt, h_gbc, h_bcc, h_small, h_same, h_taps, h_vec, h_heads, h_xin, h_cin, h_aux,
    h_ws, h_wx, h_wz,
    o_dx, o_dwx, o_dwz, o_dbc, o_ddt, o_cxw, o_cxb, o_gate, o_cbw, o_cbb, o_dtb, o_alog, o_skip, o_gain,
    normed_t, normed_far, gz, gx, gdt, gbc, bcc, bcp, same, taps, vec, heads, xin, cin, aux, w_s, w_a, w_b,
    gs, far_s, far_x, far_z, own_s, own_x, own_z,
    bufs_s, bufs_x, bufs_z, res_s, res_x, res_z,
    peer_g, relay_g, got_g, own_g, relay_bc, got_bc,
    vec_slots, gain_steps, gain_slots,
    s_ssem, s_rsem, c_ssem, c_rsem, t_ssem, t_rsem, l_sem,
):
    p = Place()
    pairs = [
        (h_gbc, gbc), (h_gz, gz), (h_gx, gx), (h_gdt, gdt), (h_ws, w_s), (h_wz, w_b), (h_wx, w_a), (h_normed_t, normed_t),
        (h_normed_far, normed_far), (h_bcc, bcc), (h_small.at[:, pl.ds(0, 128)], bcp.at[:, pl.ds(0, 128)]),
        (h_small.at[:, pl.ds(256, 128)], bcp.at[:, pl.ds(128, 128)]), (h_same, same), (h_taps, taps), (h_vec, vec.at[0]),
        (h_heads, heads), (h_xin, xin), (h_cin, cin), (h_aux, aux),
    ]
    waits = {}
    for i, (src, dst) in enumerate(pairs):
        copy = pltpu.make_async_copy(src, dst, l_sem.at[i])
        copy.start()
        waits[i] = copy
    index = {"gbc": 0, "gz": 1, "gx": 2, "gdt": 3, "ws": 4, "wz": 5, "wx": 6, "normed_t": 7, "normed_far": 8, "bcc": 9, "bcp": 10,
             "bcp_far": 11, "same": 12, "taps": 13, "vec": 14, "heads": 15, "xin": 16, "cin": 17, "aux": 18}

    def need(*names):
        for name in names:
            waits[index[name]].wait()

    p.greet(more=True)

    def columns(ref):
        return lambda h: ref.at[:, pl.ds(pl.multiple_of(h * HALF, 128), HALF)]

    sz = Scatter(p, normed_t, normed_far, columns(gz), far_z, HALF, own_z, bufs_z, res_z, s_ssem, s_rsem, 0)
    sx = Scatter(p, normed_t, normed_far, columns(gx), far_x, HALF, own_x, bufs_x, res_x, s_ssem, s_rsem, 1)
    sb = Scatter(p, normed_t, normed_far, lambda h: gs.at[h], far_s, 256, own_s, bufs_s, res_s, s_ssem, s_rsem, 2)
    cross_bc = Cross(p, relay_bc, c_ssem, c_rsem, 0)
    cross_g = Cross(p, relay_g, c_ssem, c_rsem, 1)
    total_vec = Total(p, vec, vec_slots, t_ssem, t_rsem, 0, False)
    total_gain = Total(p, gain_steps, gain_slots, t_ssem, t_rsem, 1, True)
    mine = pl.ds(pl.multiple_of(p.tz * 256, 256), 256)

    need("gbc")
    cross_bc.start(gbc.at[pl.ds(0, 256)], gbc.at[pl.ds(256, 256)])
    need("gz")
    sz.give()
    need("gx")
    sx.give()
    need("gdt", "wx", "wz", "ws")
    def share_out(value, yy, own, peer):
        cols = pl.ds(pl.multiple_of(yy * 384, 128), 384)
        low, high = value[0:256], value[256:512]
        own[:, cols] = jnp.where(p.tz == 0, low, high)
        peer[:, cols] = jnp.where(p.tz == 0, high, low).astype(BF)

    @pl.loop(0, 4)
    def _(yy):
        value = dot_nt(gdt[...], w_s[0, yy, :, :, 128:256].reshape(384, 128))
        for h in range(2):
            cols = slice(HALF * h, HALF * h + HALF)
            value += dot_nt(gz[:, cols], w_b[h, yy].reshape(384, HALF))
            value += dot_nt(gx[:, cols], w_a[h, yy].reshape(384, HALF))
        share_out(value, yy, own_g, peer_g)

    cross_g.start(peer_g.at[pl.ds(0, 128)], peer_g.at[pl.ds(128, 128)])


    need("normed_t", "normed_far")
    sz.own_half()
    cross_bc.forward(lambda t: got_bc.at[pl.ds(0, 256)], lambda t: got_bc.at[pl.ds(256, 256)])
    sx.own_half()
    cross_g.forward(lambda t: got_g.at[pl.ds(0, 128)], lambda t: got_g.at[pl.ds(128, 128)])
    sz.second()
    cross_bc.ready()
    need("heads", "bcp_far", "bcc", "bcp", "same", "taps", "vec")
    pre_bc = bcc[...]
    sigma = sig(pre_bc)
    slope = sigma * (1.0 + pre_bc * (1.0 - sigma))
    before = (gbc[...] + got_bc[...]) * slope
    inner = taps[3:4, :] * before
    vec[0, 7:8, 1024:1280] = jnp.sum(before, axis=0, keepdims=True)
    vec[0, 7:8, 1280:1408] = heads[0:1, :]
    vec[0, 7:8, 1408:1536] = heads[1:2, :]
    vec[0, 7:8, 768:1024] = jnp.sum(before * bcp[...], axis=0, keepdims=True)
    for d in (1, 2, 3):
        moved = pltpu.roll(before * same[:, d : d + 1], SEQ - d, 0)
        inner += taps[3 - d : 4 - d, :] * moved
        vec[0, 7:8, 256 * (3 - d) : 256 * (4 - d)] = jnp.sum(moved * bcp[...], axis=0, keepdims=True)
    gs[0, :, 0:128] = inner[:, :128].astype(BF)
    gs[1, :, 0:128] = inner[:, 128:].astype(BF)
    gs[0, :, 128:256] = gdt[...]
    gs[1, :, 128:256] = jnp.zeros((SEQ, 128), BF)
    sb.give()
    total_vec.start()
    @pl.loop(0, 4)
    def _(yy):
        cols = pl.ds(pl.multiple_of(yy * 384, 128), 384)
        weights = side(w_s[0, yy, :, :, 0:128].reshape(384, 128), w_s[1, yy, :, :, 0:128].reshape(384, 128))
        own_g[:, cols] += dot_nt(side(gs[0, mine, 0:128], gs[1, mine, 0:128]), weights)

    sx.second()
    sb.own_half()
    cross_g.ready()
    need("xin", "cin", "aux")
    gain = aux[0:1, :]
    sums = jnp.zeros((8, D), F32)
    for i in range(16):
        part = slice(16 * i, 16 * i + 16)
        rows = xin[part, :].astype(F32)
        inv = lax.rsqrt(jnp.mean(rows * rows, axis=-1, keepdims=True) + EPS)
        unit = rows * inv
        grad = own_g[part, :] + got_g[part, :].astype(F32)
        weighted = grad * unit
        sums += weighted.reshape(2, 8, D).sum(axis=0)
        mean = jnp.mean(weighted * gain, axis=-1, keepdims=True)
        own_g[part, :] = inv * (grad * gain - unit * mean) + cin[part, :].astype(F32)
    store_dx = pltpu.make_async_copy(own_g, o_dx, l_sem.at[len(pairs)])
    store_dx.start()
    gain_steps[0] = jnp.broadcast_to(jnp.sum(sums, axis=0, keepdims=True), (8, D))
    total_gain.start()
    sz.first_far()
    total_vec.step()
    sx.first_far()
    sz.first()
    total_gain.step()
    sb.second()
    total_vec.step()
    sx.first()
    sz.beside()
    total_gain.step()
    sb.first_far()
    total_vec.step()
    sz.home()
    sx.beside()
    total_gain.step()
    sb.first()
    total_vec.take()
    sx.home()
    total_gain.step()
    sb.beside()
    sb.home()
    total_gain.take()
    done = vec[4]
    o_cxw[...] = done[0:4]
    o_cxb[...] = done[4:5]
    o_gate[...] = done[5:6]
    channel = lax.broadcasted_iota(jnp.int32, (D, 128), 0)
    head = lax.broadcasted_iota(jnp.int32, (D, 128), 1)
    pick = (channel // 64 == head).astype(F32).astype(BF)
    skips = dot(side(*split(jnp.broadcast_to(done[6:7], (8, D)))), below(pick, pick))
    o_skip[...] = skips[0:1, 0:24]
    o_dtb[...] = done[7:8, 1280:1304]
    o_alog[...] = done[7:8, 1408:1432]
    rank = p.dp * 2 + p.tz
    for k in range(5):
        moved = pltpu.roll(done[:, 256 * k : 256 * k + 256], (256 - 2 * rank) % 256, 1)
        if k < 4:
            o_cbw[k : k + 1, :] = moved[7:8, 0:2]
        else:
            o_cbb[...] = moved[7:8, 0:2]
    o_gain[...] = pltpu.roll(gain_steps[5], (D - 12 * rank) % D, 1)[0:1, 0:12]
    results = [(res_x, o_dwx), (res_z, o_dwz)]
    for scatter in (sz, sx, sb):
        scatter.finish()
    both = side(res_s[:, 0:128], res_s[:, 256:384])
    o_dbc[...] = jnp.where(p.tz == 0, both, pltpu.roll(both, 12, 0))[0:12]
    o_ddt[...] = res_s[:, 128:152]
    stores = []
    for i, (src, dst) in enumerate(results):
        copy = pltpu.make_async_copy(src, dst, l_sem.at[len(pairs) + 1 + i])
        copy.start()
        stores.append(copy)
    cross_bc.release()
    cross_g.release()
    for cross in (cross_bc, cross_g):
        cross.finish()
    total_vec.finish()
    total_gain.finish()
    store_dx.wait()
    for copy in stores:
        copy.wait()


def back(args):
    any_space = pl.BlockSpec(memory_space=pl.ANY)
    sds = jax.ShapeDtypeStruct
    vmem = pl.BlockSpec(memory_space=pltpu.VMEM)
    piece = sds((24, D), F32)
    small = [(12, 256), (24, 24), (4, D), (1, D), (1, D), (4, 2), (1, 2), (1, 24), (1, 24), (1, 24), (1, 12)]
    outs = [sds((256, D), F32), piece, piece] + [sds(s, F32) for s in small]

    half = lambda w: pltpu.VMEM((4, 4, 96, w), BF)
    wide = pltpu.VMEM((2, 4, 4, 96, HALF), BF)
    rows = lambda n, t: pltpu.VMEM((n, D), t)
    scratch = [
        pltpu.VMEM((D, SEQ), BF), pltpu.VMEM((D, SEQ), BF), rows(SEQ, BF), rows(SEQ, BF),
        pltpu.VMEM((SEQ, 128), BF), pltpu.VMEM((SEQ, 256), F32), pltpu.VMEM((SEQ, 256), F32), pltpu.VMEM((SEQ, 256), F32),
        pltpu.VMEM((SEQ, 128), F32), pltpu.VMEM((8, 256), F32), pltpu.VMEM((5, 8, D), F32), pltpu.VMEM((8, 128), F32),
        rows(256, BF), rows(256, BF), rows(8, F32), pltpu.VMEM((2, 4, 4, 96, 256), BF), wide, wide,
        pltpu.VMEM((2, SEQ, 256), BF), pltpu.VMEM((SEQ, 256), BF), pltpu.VMEM((SEQ, HALF), BF), pltpu.VMEM((SEQ, HALF), BF),
        half(256), half(HALF), half(HALF),
        bufs(256), bufs(HALF), bufs(HALF),
        pltpu.VMEM((24, 512), F32), rows(24, F32), rows(24, F32),
        rows(256, BF), pltpu.VMEM((2, 128, D), BF), rows(256, BF), rows(256, F32),
        pltpu.VMEM((2, 256, 256), F32), pltpu.VMEM((SEQ, 256), F32),
        pltpu.VMEM((8, 8, D), F32), pltpu.VMEM((6, 8, D), F32), pltpu.VMEM((9, 8, D), F32),
        pltpu.SemaphoreType.DMA((3, Scatter.COUNT)), pltpu.SemaphoreType.DMA((3, Scatter.COUNT)),
        pltpu.SemaphoreType.DMA((2, 4)), pltpu.SemaphoreType.DMA((2, 4)),
        pltpu.SemaphoreType.DMA((2, Total.COUNT)), pltpu.SemaphoreType.DMA((2, Total.COUNT)),
        pltpu.SemaphoreType.DMA((32,)),
    ]
    return pl.pallas_call(
        back_kernel,
        out_shape=outs,
        in_specs=[any_space] * len(args),
        out_specs=[any_space] * 3 + [vmem] * len(small),
        scratch_shapes=scratch,
        compiler_params=pltpu.CompilerParams(collective_id=1, has_side_effects=True, vmem_limit_bytes=63 * 1024 * 1024),
        cost_estimate=pl.CostEstimate(flops=2 * SEQ * D * 10240, bytes_accessed=50_000_000, transcendentals=0),
    )(*args)


def settle_kernel(count, *refs):
    for i in range(count):
        refs[count + i][...] = refs[i][...]


def settle(results):
    specs = [pl.BlockSpec(memory_space=pltpu.VMEM)] * len(results)
    return pl.pallas_call(
        functools.partial(settle_kernel, len(results)),
        out_shape=[jax.ShapeDtypeStruct(v.shape, v.dtype) for v in results],
        in_specs=specs,
        out_specs=specs,
        compiler_params=pltpu.CompilerParams(vmem_limit_bytes=62 * 1024 * 1024),
    )(*results)


def per_device(
    block_input, cotangent, seg_ids, norm_gain, w_z, w_x, w_bc, w_dt, conv_x_w, conv_x_b, conv_bc_w, conv_bc_b,
    dt_bias, a_log, d_skip, gate_gain, w_out,
):
    tz = lax.axis_index("tensor")
    first = (tz == 0).astype(F32)
    conv = jnp.pad(conv_bc_w.astype(F32).T, ((0, 0), (0, 1))) + jnp.pad(conv_bc_b.astype(F32)[:, None], ((0, 0), (4, 0)))
    own = jnp.pad(w_bc.astype(F32), ((0, 0), (0, 256)))
    own = own + jnp.pad(norm_gain.astype(F32)[:, None], ((0, 0), (256, 255))) + jnp.pad(conv, ((0, 10), (257, 250)))
    tiny = jnp.pad(own * first, ((0, 12), (0, 0))) + jnp.pad(own * (1.0 - first), ((12, 0), (0, 0)))
    tiny = tiny + jnp.pad(w_dt.astype(F32), ((0, 0), (384, 104)))
    segr = jnp.broadcast_to(seg_ids.astype(F32)[None, :], (8, SEQ))
    put = lambda v, row, lane: jnp.pad(v.astype(F32)[None], ((row, 7 - row), (lane, D - lane - v.shape[0])))
    chan_in = jnp.pad(conv_x_w.astype(F32), ((0, 4), (0, 0))) + put(conv_x_b, 4, 0) + put(gate_gain, 5, 0)
    chan_in = chan_in + put(dt_bias, 6, 0) + put(a_log, 6, 128) + put(d_skip, 6, 256)
    (
        normed_t, cot_t, x_pre, z_part, grad_mixed, small, aux, ws, wx, wz, wo,
        xcp, y_low, sums, bcc, bc, cum, cum_t, step, same, segc, taps, chans, heads, mixed, normed_far, cot_far,
    ) = front((w_x, w_z, w_out.T, tiny, segr, chan_in, block_input, cotangent))
    gz, gx, vec, gbc, gdt, d_heads, dwo, out = scan_backward(
        (x_pre, z_part, grad_mixed, xcp, y_low, sums, small, same, segc, segr, chans, heads, bc, cum, cum_t, step),
        (mixed, cot_t, cot_far, wo, block_input),
    )
    results = back(
        (normed_t, normed_far, gz, gx, gdt, gbc, bcc, small, same, taps, vec, d_heads, block_input, cotangent, aux, ws, wx, wz)
    )
    out, dwo, d_x, dwx, dwz, d_bc, d_dt, cxw, cxb, d_gate, cbw, cbb, d_bias, d_rate, d_skips, gain = settle([out, dwo, *results])
    flat = lambda v: v.reshape(v.shape[1])
    return (
        out, d_x, flat(gain), dwz, dwx, d_bc, d_dt, cxw, flat(cxb), cbw, flat(cbb), flat(d_bias), flat(d_rate), flat(d_skips),
        flat(d_gate), dwo.T,
    )


def solution(mesh):
    both = ("dp", "tensor")
    in_specs = (
        P(both, None), P(both, None), P("dp"), P(both), P("dp", "tensor"), P("dp", "tensor"), P(both, None), P("dp", "tensor"),
        P(None, "tensor"), P("tensor"), P(None, both), P(both), P("tensor"), P("tensor"), P("tensor"), P("tensor"),
        P("tensor", "dp"),
    )
    out_specs = (
        P(both, None), P(both, None), P(both), P("dp", "tensor"), P("dp", "tensor"), P(both, None), P("dp", "tensor"),
        P(None, "tensor"), P("tensor"), P(None, both), P(both), P("tensor"), P("tensor"), P("tensor"), P("tensor"),
        P("tensor", "dp"),
    )
    return jax.shard_map(per_device, mesh=mesh, in_specs=in_specs, out_specs=out_specs, check_vma=False)
```
